32 devices in a mesh: groups: 1, expert: 16 (over z, y, core), head: 2 (over x).
Axes of the slice: x: 2, y: 2, z: 4, core: 2. Of those that a mesh axis runs over, the one named last changes fastest.
Arguments:
- tokens: bfloat16 [4096, 1024], P(('groups', 'expert')), may hold values from -6 to 6
- router: bfloat16 [1024, 16], replicated, may hold values from -0.1875 to 0.1875
- routes: int32 [4096, 2], P(('groups', 'expert')), may hold values from 0 to 15, all different within a row; in each aligned block of 256 rows (0 to 255, 256 to 511, ...) at most 48 rows name the same one
- w_in: bfloat16 [16, 1024, 4096], P('expert', None, 'head'), may hold values from -0.1875 to 0.1875
- w_out: bfloat16 [16, 4096, 1024], P('expert', 'head'), may hold values from -0.125 to 0.125
- lengths: int32 [32], P(('groups', 'expert')), may hold values from 1 to 128, 3072 in all
- kv_weight: bfloat16 [1024, 2, 1024], P('expert', None, 'head'), may hold values from -0.1875 to 0.1875
Outputs:
- kv: bfloat16 [4096, 2, 1024], P(('groups', 'expert'), None, 'head')
The draws below stay inside these ranges and needn't reach their ends.
Inputs may be any that keep to these rules, and one draw needn't show every extreme that they name: `routes`: each row names two different experts; within the rows of one index of expert, aligned blocks of 256 rows, no expert is named more than 48 times, a bound that some block reaches. The lengths sum to 3072 and the largest is exactly 128.
All inputs are finite; a program needn't handle non-finite values. No bound on the sum of `lengths` on one device may be relied on, other than what follows from the above.
Results may differ from the reference program's by a relative error of at most 0.019.
Values may be sent and summed in bfloat16 or wider, within the bound.
A program may use at most 64 MiB of HBM per device.

```python
import math
import jax
import jax.numpy as jnp
import numpy as np
from jax import lax

D = 1024
FF = 4096
QCOL = 256
SLEN = 128
TOK_DEV = 256
EXPERTS = 16
CAP = 48
SENTS = 32
TOKENS = 4096


def strengthened(array, rng, source, target, shards_of, factor):
    owner, partner = [(jnp.arange(array.shape[dim]) // (array.shape[dim] // shards_of)).reshape([-1 if axis == dim else 1 for axis in range(array.ndim)]) for dim in (source, target)]
    chosen = jax.random.permutation(rng, shards_of)[partner]
    strong = (owner == chosen) | (owner == (partner + shards_of // 2) % shards_of)
    return jnp.where(strong, factor * array, array)


def steps_of(own_key, extent, cuts, low, largest):
    factor_of = 1.0
    for dim, parts in cuts:
        steps = jax.random.uniform(jax.random.fold_in(jax.random.fold_in(own_key, 6), dim), (parts,), jnp.float32, low / len(cuts), largest / len(cuts))
        factor_of = factor_of * jnp.repeat(jnp.exp(steps), extent[dim] // parts).reshape((-1,) + (1,) * (len(extent) - 1 - dim))
    return factor_of


def profile(count, total, reach, lean):
    weights = [(1 << 20) // math.isqrt(grade ** lean) + 1 for grade in range(2, count + 1)]
    rest, counts = total - reach - (count - 1), [1] * (count - 1)
    while rest > 0:
        candidates = [i for i in range(count - 1) if counts[i] < reach]
        mass, remaining = sum([weights[i] for i in candidates]), rest
        for i in candidates:
            more = min(reach - counts[i], max(1, remaining * weights[i] // mass), rest)
            counts[i] = counts[i] + more
            rest = rest - more
    return np.array([reach] + counts)


def ragged(own_key, count, total, reach, slope):
    if count == 2:
        one = jax.random.randint(own_key, (), max(1, total - reach), min(reach, total - 1) + 1)
        return jnp.stack([one, total - one])
    sizes = jnp.asarray(profile(count, total, reach, slope), jnp.int32)
    pairs = (count - 1) // 2
    giver, taker = sizes[1:1 + 2 * pairs:2], sizes[2:2 + 2 * pairs:2]
    slack = jnp.minimum(giver - 1, reach - taker)
    moved = jax.random.randint(jax.random.fold_in(own_key, 1), (pairs,), 0, 1 << 20) % (slack + 1)
    sizes = sizes.at[1:1 + 2 * pairs:2].set(giver - moved).at[2:2 + 2 * pairs:2].set(taker + moved)
    return sizes[jax.random.permutation(jax.random.fold_in(own_key, 2), count)]


def routed_block(key, own, number, rows, number_of, top, most, lean):
    order = jax.random.permutation(key, number_of)
    heavy_load, usual = portions_of(number_of, rows * top, most, lean, True), portions_of(number_of, rows * top, most, lean, False)
    places = jnp.arange(number_of)

    def named(tallies, rotation):
        used = int((tallies > 0).sum())
        fixed = max(1, used // 4)
        shifted = fixed + (places - fixed + rotation * (used - fixed)) % max(1, number_of - fixed)
        return jnp.zeros((number_of,), jnp.int32).at[order[jnp.where(places < fixed, places, shifted)]].set(jnp.asarray(tallies, jnp.int32))

    tallies = jnp.where(number % 4 == 0, named(heavy_load, number // 4), named(usual, number - number // 4 - 1))
    mixed = jax.random.permutation(jax.random.fold_in(own, 3), number_of)
    donor, sink = mixed[0:number_of // 2 * 2:2], mixed[1:number_of // 2 * 2:2]
    room = jnp.minimum(tallies[donor] - 1, most - tallies[sink]) // 2
    room = jnp.where((donor == order[0]) | (sink == order[0]) | (tallies[sink] == 0), 0, jnp.maximum(room, 0))
    shifted = jax.random.randint(jax.random.fold_in(own, 4), (number_of // 2,), 0, 1 << 20) % (room + 1)
    tallies = tallies.at[donor].add(-shifted).at[sink].add(shifted)
    items = jnp.searchsorted(jnp.cumsum(tallies), jnp.arange(rows * top), side="right").astype(jnp.int32)
    listing = items.reshape(top, rows).T
    listing = listing[jax.random.permutation(jax.random.fold_in(own, 1), rows)]
    rotation = jax.random.randint(jax.random.fold_in(own, 2), (rows, 1), 0, top)
    return jnp.take_along_axis(listing, (jnp.arange(top)[None, :] + rotation) % top, axis=1)


def portions_of(amount, total, most, skew, full):
    loads = [(1 << 20) // math.isqrt(grade ** skew) + 1 for grade in range(1, amount + 1)]
    largest = most if full else min(most, max(-(-total // amount), total * loads[0] // sum(loads)))
    least = 1 if total - largest >= amount - 1 else 0
    holding, spare = [largest] + [least] * (amount - 1), total - largest - least * (amount - 1)
    while spare > 0:
        movable = [i for i in range(1, amount) if holding[i] < largest] or [i for i in range(1, amount) if holding[i] < most]
        whole, remaining = sum([loads[i] for i in movable]), spare
        for i in movable:
            addition = min(most - holding[i], max(1, remaining * loads[i] // whole), spare)
            holding[i] = holding[i] + addition
            spare = spare - addition
    return np.array(holding)


def normal_values(stream_key, shape, scale, bound, shards=(), held_as=jnp.bfloat16):
    values = jax.random.normal(stream_key, shape, jnp.float32) * scale
    if len(shards) > 0:
        values = steps_of(stream_key, shape, shards, -0.22, 0.18) * values
    return jnp.clip(values, min=-bound, max=bound).astype(held_as)


def bell_draw_with(stream_key, shape, scale, most, shards, heavy, kind=jnp.bfloat16):
    values = scale * jax.random.normal(stream_key, shape, jnp.float32)
    if shards:
        values = values * steps_of(stream_key, shape, shards, -0.22, 0.18)
    return jnp.clip(strengthened(values, jax.random.fold_in(stream_key, 3), *heavy), -most, most).astype(kind)


def setup_inputs(seed: int = 0, part: int = 0) -> dict:
    key_list = jax.random.split(jax.random.key(seed), 8)
    part_splits = jax.random.split(jax.random.fold_in(key_list[7], part), 8)
    tokens = normal_values(part_splits[0], (TOKENS, D), 1.0, 6.0, ((0, 16),))
    router = normal_values(key_list[1], (D, EXPERTS), D ** -0.5, 0.1875)
    routes_keys = jax.random.split(jax.random.fold_in(part_splits[2], 1), TOKENS // TOK_DEV)
    routes_turns = jax.random.permutation(jax.random.fold_in(part_splits[2], 3), TOKENS // TOK_DEV)
    routes = jax.vmap(lambda own, number: routed_block(jax.random.fold_in(part_splits[2], 2), own, number, TOK_DEV, EXPERTS, 2, CAP, 1))(routes_keys, routes_turns).reshape((TOKENS, 2))
    w_in = normal_values(key_list[3], (EXPERTS, D, FF), D ** -0.5, 0.1875, ((0, 16), (2, 2)))
    w_out = bell_draw_with(key_list[4], (EXPERTS, FF, D), FF ** -0.5, 0.125, ((0, 16), (1, 2)), (1, 2, 2, 2.0))
    lengths = ragged(part_splits[5], SENTS, 3 * SENTS * SLEN // 4, SLEN, 2).astype(jnp.int32)
    kv_weight = normal_values(key_list[6], (D, 2, D), D ** -0.5, 0.1875, ((0, 16), (2, 2)))
    return {"tokens": tokens, "router": router, "routes": routes, "w_in": w_in, "w_out": w_out, "lengths": lengths, "kv_weight": kv_weight}


def layer_norm(values):
    wide = values.astype(jnp.float32)
    center = lax.optimization_barrier(jnp.mean(wide, axis=-1, keepdims=True))
    spread = lax.optimization_barrier(jnp.mean((wide - center) ** 2, axis=-1, keepdims=True))
    return ((wide - center) * lax.rsqrt(spread + 1e-05)).astype(jnp.bfloat16)

def reference(tokens, router, routes, w_in, w_out, lengths, kv_weight):
    blocks = TOKENS // TOK_DEV
    normed = layer_norm(tokens)
    logits = jnp.dot(normed, router, preferred_element_type=jnp.float32)
    chosen = jnp.take_along_axis(logits, routes, axis=1)
    first = 1.0 / (1.0 + jnp.exp(chosen[:, 1] - chosen[:, 0]))
    gates = jnp.stack([first, 1.0 - first], axis=1)
    flat_ids = routes.reshape(blocks, TOK_DEV * 2)
    onehot = (flat_ids[:, :, None] == jnp.arange(EXPERTS, dtype=jnp.int32)[None, None, :]).astype(jnp.int32)
    before = jnp.cumsum(onehot, axis=1) - onehot
    slot = lax.optimization_barrier(jnp.sum(before * onehot, axis=2)).astype(jnp.int32)
    block_of = jnp.broadcast_to(jnp.arange(blocks, dtype=jnp.int32)[:, None], (blocks, TOK_DEV * 2))
    position = ((flat_ids * blocks + block_of) * CAP + slot).reshape(-1).astype(jnp.int32)
    repeated = jnp.repeat(normed, 2, axis=0)
    buffer = jnp.zeros((EXPERTS * blocks * CAP, D), jnp.bfloat16).at[position].set(repeated)
    buffer = buffer.reshape(EXPERTS, blocks * CAP, D)

    def one_expert(items):
        rows, first_w, second_w = items
        hidden = jax.nn.relu(jnp.dot(rows, first_w, preferred_element_type=jnp.float32)).astype(jnp.bfloat16)
        return jnp.dot(hidden, second_w, preferred_element_type=jnp.float32).astype(jnp.bfloat16)
    expert_out = lax.map(one_expert, (buffer, w_in, w_out)).reshape(EXPERTS * blocks * CAP, D)
    picked = expert_out[position].reshape(TOKENS, 2, D).astype(jnp.float32)
    encoded = tokens.astype(jnp.float32) + lax.optimization_barrier(jnp.sum(gates[:, :, None] * picked, axis=1))
    grouped = encoded.reshape(TOKENS, D // QCOL, QCOL)
    scales = (lax.optimization_barrier(jnp.max(jnp.abs(grouped), axis=2)) / 127.0 + 1e-06).astype(jnp.bfloat16)
    coded = jnp.floor(grouped / scales.astype(jnp.float32)[:, :, None] + 0.5)
    scaled = jnp.clip(coded, -127.0, 127.0).astype(jnp.bfloat16)
    restored = (scaled.astype(jnp.float32) * scales.astype(jnp.float32)[:, :, None]).astype(jnp.bfloat16)
    restored = restored.reshape(TOKENS, D)
    projected = jnp.einsum('td,dcj->tcj', restored.astype(jnp.float32), kv_weight.astype(jnp.float32))
    place = jnp.arange(TOKENS, dtype=jnp.int32)
    limit = lengths[place // SLEN]
    keep = (place % SLEN < limit).astype(jnp.float32)
    return (projected * keep[:, None, None]).astype(jnp.bfloat16)
```

```python
import functools

import jax
import jax.numpy as jnp
from jax import lax
from jax.experimental import pallas as pl
from jax.experimental.pallas import tpu as pltpu
from jax.sharding import PartitionSpec as P

QCOL = 256
SLEN = 128
MESH = pl.DeviceIdType.MESH
F32 = jnp.float32
BF16 = jnp.bfloat16


def flip(me, k, n):
    out, bit = 0, 1
    while bit < n:
        a = lax.rem(lax.div(me, jnp.int32(bit)), jnp.int32(2))
        b = lax.rem(lax.div(jnp.int32(k), jnp.int32(bit)), jnp.int32(2))
        out = out + bit * lax.rem(a + b, jnp.int32(2))
        bit *= 2
    return out


def kernel(
    n, cap, groups,
    tokens_ref, router_ref, routes_ref, w_in_hbm, w_out_hbm, restored_ref,
    w_in, w_out, onehots, outgoing, rows_in, hidden, part_out, part_in, part_own, summed, back, coded,
    w_sem, disp_send, disp_recv, fwd_send, fwd_recv, red_send, red_recv, ret_send, ret_recv, code_send, code_recv,
):
    me = lax.axis_index("expert")
    head = lax.axis_index("head")
    other = 1 - head
    count, width = tokens_ref.shape
    half = width // 2
    ff = w_in.shape[1]
    block = n // groups * cap
    near = n // 2
    mine = pl.ds(pl.multiple_of(head * half, half), half)
    theirs = pl.ds(pl.multiple_of(other * half, half), half)

    load_in = pltpu.make_async_copy(w_in_hbm.at[0], w_in, w_sem.at[0])
    load_out = pltpu.make_async_copy(w_out_hbm.at[0], w_out, w_sem.at[1])
    load_in.start()
    load_out.start()

    barrier = pltpu.get_barrier_semaphore()

    @pl.loop(1, n)
    def _(k):
        pl.semaphore_signal(barrier, inc=1, device_id={"expert": flip(me, k, n)}, device_id_type=MESH)

    pl.semaphore_signal(barrier, inc=1, device_id={"head": other}, device_id_type=MESH)

    wide = tokens_ref[...].astype(F32)
    center = jnp.mean(wide, axis=-1, keepdims=True)
    spread = jnp.mean((wide - center) ** 2, axis=-1, keepdims=True)
    normed = ((wide - center) * lax.rsqrt(spread + 1e-05)).astype(BF16)
    logits = jnp.dot(normed, router_ref[...], preferred_element_type=F32)
    route0 = routes_ref[:, 0:1]
    route1 = routes_ref[:, 1:2]
    ids = lax.broadcasted_iota(jnp.int32, (count, n), 1)
    hot0 = (ids == route0).astype(F32)
    hot1 = (ids == route1).astype(F32)
    earlier = (
        lax.broadcasted_iota(jnp.int32, (count, count), 1) < lax.broadcasted_iota(jnp.int32, (count, count), 0)
    ).astype(F32).astype(BF16)
    before = jnp.dot(earlier, (hot0 + hot1).astype(BF16), preferred_element_type=F32)
    slot0 = jnp.sum(before * hot0, axis=1, keepdims=True).astype(jnp.int32)
    slot1 = jnp.sum(before * hot1, axis=1, keepdims=True).astype(jnp.int32)
    chosen0 = jnp.sum(logits * hot0, axis=1, keepdims=True)
    chosen1 = jnp.sum(logits * hot1, axis=1, keepdims=True)
    gate0 = 1.0 / (1.0 + jnp.exp(chosen1 - chosen0))
    gate1 = 1.0 - gate0
    place0 = jnp.bitwise_xor(route0, me) * cap + slot0
    place1 = jnp.bitwise_xor(route1, me) * cap + slot1
    columns = lax.broadcasted_iota(jnp.int32, (count, n * cap), 1)
    at0 = columns == place0
    at1 = columns == place1
    onehots[...] = jnp.where(at0 | at1, 1.0, 0.0).astype(BF16)

    def packed(first, last):
        picks = onehots[:, first * cap : last * cap]
        outgoing[first * cap : last * cap, :] = lax.dot_general(
            picks, normed, (((0,), (0,)), ((), ())), preferred_element_type=F32
        ).astype(BF16)

    def at(k):
        return pl.ds(pl.multiple_of(k * cap, cap), cap)

    def far_copy(k):
        return pltpu.make_async_remote_copy(
            src_ref=outgoing.at[at(k), mine], dst_ref=rows_in.at[at(k), mine],
            send_sem=disp_send.at[k], recv_sem=disp_recv.at[k],
            device_id={"expert": flip(me, k, n)}, device_id_type=MESH,
        )

    def near_copy(k):
        return pltpu.make_async_remote_copy(
            src_ref=outgoing.at[at(k)], dst_ref=rows_in.at[at(k)],
            send_sem=disp_send.at[k], recv_sem=disp_recv.at[k],
            device_id={"expert": flip(me, k, n)}, device_id_type=MESH,
        )

    packed(near, n)
    pl.semaphore_wait(barrier, n)

    @pl.loop(near, n)
    def _(k):
        far_copy(k).start()

    packed(0, near)

    @pl.loop(1, near)
    def _(k):
        near_copy(k).start()

    rows_in[0:cap, :] = outgoing[0:cap, :]

    low = jnp.where(at0, gate0, jnp.where(at1, gate1, 0.0))
    onehots[...] = low.astype(BF16)
    rest = (low - low.astype(BF16).astype(F32)).astype(BF16)

    per = n // groups

    def span(g):
        return slice(g * block, (g + 1) * block)

    def forward_copy(g):
        return pltpu.make_async_remote_copy(
            src_ref=rows_in.at[span(g), mine], dst_ref=rows_in.at[span(g), mine],
            send_sem=fwd_send.at[g], recv_sem=fwd_recv.at[g],
            device_id={"head": other}, device_id_type=MESH,
        )

    def reduce_copy(g):
        return pltpu.make_async_remote_copy(
            src_ref=part_out.at[span(g)], dst_ref=part_in.at[span(g)],
            send_sem=red_send.at[g], recv_sem=red_recv.at[g],
            device_id={"head": other}, device_id_type=MESH,
        )

    def return_copy(k):
        return pltpu.make_async_remote_copy(
            src_ref=summed.at[at(k)], dst_ref=back.at[at(k)],
            send_sem=ret_send.at[k], recv_sem=ret_recv.at[k],
            device_id={"expert": flip(me, k, n)}, device_id_type=MESH,
        )

    def arrive(g):
        far = g * per >= near

        @pl.loop(max(1, g * per), (g + 1) * per)
        def _(k):
            (far_copy if far else near_copy)(k).wait_recv()

        if far:
            forward_copy(g).start()

    def work(g):
        if g == 0:
            load_in.wait()
        if g * per >= near:
            forward_copy(g).wait_recv()
        tile = ff // 4

        @pl.loop(0, 4)
        def _(i):
            cols = pl.ds(pl.multiple_of(i * tile, tile), tile)
            value = jnp.dot(rows_in[span(g), :], w_in[:, cols], preferred_element_type=F32)
            hidden[:, cols] = jnp.maximum(value, 0.0).astype(BF16)

        if g == 0:
            load_out.wait()
        part_out[span(g), :] = jnp.dot(hidden[...], w_out[:, theirs], preferred_element_type=F32).astype(BF16)
        reduce_copy(g).start()
        part_own[span(g), :] = jnp.dot(hidden[...], w_out[:, mine], preferred_element_type=F32)

    def give(g):
        reduce_copy(g).wait_recv()
        summed[span(g), :] = (part_own[span(g), :] + part_in[span(g), :].astype(F32)).astype(BF16)
        if g == 0:
            back[0:cap, :] = summed[0:cap, :]

        @pl.loop(max(1, g * per), (g + 1) * per)
        def _(k):
            return_copy(k).start()

    arrive(0)
    work(0)
    arrive(1)
    for g in range(1, groups):
        if g + 1 < groups:
            arrive(g + 1)
        work(g)
        give(g - 1)
    give(groups - 1)

    @pl.loop(1, n)
    def _(k):
        return_copy(k).wait_recv()

    encoded = (
        tokens_ref[:, mine].astype(F32)
        + jnp.dot(onehots[...], back[...], preferred_element_type=F32)
        + jnp.dot(rest, back[...], preferred_element_type=F32)
    )
    for q in range(half // QCOL):
        part = encoded[:, q * QCOL : (q + 1) * QCOL]
        scale = (jnp.max(jnp.abs(part), axis=1, keepdims=True) / 127.0 + 1e-06).astype(BF16).astype(F32)
        whole = jnp.clip(jnp.floor(part / scale + 0.5), -127.0, 127.0)
        cols = pl.ds(pl.multiple_of(head * half + q * QCOL, QCOL), QCOL)
        coded[:, cols] = (whole * scale).astype(BF16)
    swap = pltpu.make_async_remote_copy(
        src_ref=coded.at[:, mine], dst_ref=coded.at[:, mine],
        send_sem=code_send, recv_sem=code_recv,
        device_id={"head": other}, device_id_type=MESH,
    )
    swap.start()

    @pl.loop(1, near)
    def _(k):
        near_copy(k).wait_send()

    @pl.loop(near, n)
    def _(k):
        far_copy(k).wait_send()

    @pl.loop(1, n)
    def _(k):
        return_copy(k).wait_send()

    for g in range(groups):
        if g * per >= near:
            forward_copy(g).wait_send()
        reduce_copy(g).wait_send()
    swap.wait()
    restored_ref[...] = coded[...]


def encoder(tokens, router, routes, w_in, w_out):
    n = lax.axis_size("expert")
    count, width = tokens.shape
    half = width // 2
    ff = w_in.shape[2]
    cap = -(-(3 * count // n) // 16) * 16
    groups = 4
    slots = n * cap
    vmem = pl.BlockSpec(memory_space=pltpu.VMEM)
    anywhere = pl.BlockSpec(memory_space=pl.ANY)
    dma = pltpu.SemaphoreType.DMA
    return pl.pallas_call(
        functools.partial(kernel, n, cap, groups),
        out_shape=jax.ShapeDtypeStruct((count, width), BF16),
        in_specs=[vmem, vmem, vmem, anywhere, anywhere],
        out_specs=vmem,
        scratch_shapes=[
            pltpu.VMEM((width, ff), BF16),
            pltpu.VMEM((ff, width), BF16),
            pltpu.VMEM((count, slots), BF16),
            pltpu.VMEM((slots, width), BF16),
            pltpu.VMEM((slots, width), BF16),
            pltpu.VMEM((slots // groups, ff), BF16),
            pltpu.VMEM((slots, half), BF16),
            pltpu.VMEM((slots, half), BF16),
            pltpu.VMEM((slots, half), F32),
            pltpu.VMEM((slots, half), BF16),
            pltpu.VMEM((slots, half), BF16),
            pltpu.VMEM((count, width), BF16),
            dma((2,)),
            dma((n,)), dma((n,)),
            dma((groups,)), dma((groups,)),
            dma((groups,)), dma((groups,)),
            dma((n,)), dma((n,)),
            dma, dma,
        ],
        compiler_params=pltpu.CompilerParams(
            collective_id=0, has_side_effects=True, vmem_limit_bytes=58 * 1024 * 1024
        ),
        cost_estimate=pl.CostEstimate(
            flops=4 * slots * width * ff, bytes_accessed=4 * width * ff, transcendentals=0
        ),
    )(tokens, router, routes, w_in, w_out)


def body(tokens, router, routes, w_in, w_out, lengths, kv_weight):
    count = tokens.shape[0]
    weight = lax.all_gather(kv_weight, "expert", axis=0, tiled=True)
    restored = encoder(tokens, router, routes, w_in, w_out)
    projected = jnp.einsum("td,dcj->tcj", restored, weight, preferred_element_type=F32)
    place = jnp.arange(count, dtype=jnp.int32)
    sentence = place // SLEN
    pick_len = (sentence[:, None] == jnp.arange(lengths.shape[0], dtype=jnp.int32)[None, :]).astype(
        jnp.int32
    )
    limit = jnp.sum(pick_len * lengths[None, :], axis=1)
    keep = (place % SLEN < limit).astype(F32)
    return (projected * keep[:, None, None]).astype(BF16)


def solution(mesh):
    placed = (
        P(("groups", "expert"), None),
        P(),
        P(("groups", "expert"), None),
        P("expert", None, "head"),
        P("expert", "head", None),
        P(("groups", "expert")),
        P("expert", None, "head"),
    )
    return jax.shard_map(
        body,
        mesh=mesh,
        in_specs=placed,
        out_specs=P(("groups", "expert"), None, "head"),
        check_vma=False,
    )
```

```python
import functools

import jax
import jax.numpy as jnp
from jax import lax
from jax.experimental import pallas as pl
from jax.experimental.pallas import tpu as pltpu
from jax.sharding import PartitionSpec as P

QCOL = 256
SLEN = 128
MESH = pl.DeviceIdType.MESH
F32 = jnp.float32
BF16 = jnp.bfloat16


def flip(me, k, n):
    out, bit = 0, 1
    while bit < n:
        a = lax.rem(lax.div(me, jnp.int32(bit)), jnp.int32(2))
        b = lax.rem(lax.div(jnp.int32(k), jnp.int32(bit)), jnp.int32(2))
        out = out + bit * lax.rem(a + b, jnp.int32(2))
        bit *= 2
    return out


def kernel(
    n, cap, spans,
    tokens_ref, router_ref, routes_ref, lengths_ref, kv_hbm, w_in_hbm, w_out_hbm, kv_ref,
    w_in, w_out, onehots, outgoing, rows_in, hidden, part_out, part_in, part_own, summed, back, coded, kv_all, part_kv,
    w_sem, disp_send, disp_recv, fwd_send, fwd_recv, red_send, red_recv, ret_send, ret_recv, code_send, code_recv, kv_send, kv_recv,
):
    me = lax.axis_index("expert")
    head = lax.axis_index("head")
    other = 1 - head
    count, width = tokens_ref.shape
    half = width // 2
    ff = w_in.shape[1]
    groups = len(spans)
    depth = kv_hbm.shape[0]
    near = n // 2
    mine = pl.ds(pl.multiple_of(head * half, half), half)
    theirs = pl.ds(pl.multiple_of(other * half, half), half)

    load_in = pltpu.make_async_copy(w_in_hbm.at[0], w_in, w_sem.at[0])
    load_out = pltpu.make_async_copy(w_out_hbm.at[0], w_out, w_sem.at[1])

    def kv_at(expert):
        return pl.ds(pl.multiple_of(expert * depth, depth), depth)

    load_kv = pltpu.make_async_copy(kv_hbm, kv_all.at[kv_at(me)], w_sem.at[2])
    load_kv.start()
    load_in.start()
    load_out.start()

    barrier = pltpu.get_barrier_semaphore()

    @pl.loop(1, n)
    def _(k):
        pl.semaphore_signal(barrier, inc=1, device_id={"expert": flip(me, k, n)}, device_id_type=MESH)

    pl.semaphore_signal(barrier, inc=1, device_id={"head": other}, device_id_type=MESH)

    load_kv.wait()
    pl.semaphore_wait(barrier, n)

    def kv_copy(bit, i):
        owner = flip(me, i * (2 * bit), n)
        sem = n // (2 * bit) - 1 + i
        return pltpu.make_async_remote_copy(
            src_ref=kv_all.at[kv_at(owner)], dst_ref=kv_all.at[kv_at(owner)],
            send_sem=kv_send.at[sem], recv_sem=kv_recv.at[sem],
            device_id={"expert": flip(me, bit, n)}, device_id_type=MESH,
        )

    def kv_start(bit):
        @pl.loop(0, n // (2 * bit))
        def _(i):
            kv_copy(bit, i).start()

    def kv_wait(bit):
        @pl.loop(0, n // (2 * bit))
        def _(i):
            kv_copy(bit, i).wait_recv()

    bits = []
    while n >> (len(bits) + 1):
        bits.append(n >> (len(bits) + 1))
    kv_start(bits[0])

    wide = tokens_ref[...].astype(F32)
    center = jnp.mean(wide, axis=-1, keepdims=True)
    spread = jnp.mean((wide - center) ** 2, axis=-1, keepdims=True)
    normed = ((wide - center) * lax.rsqrt(spread + 1e-05)).astype(BF16)
    logits = lax.dot_general(normed, router_ref[...], (((1,), (1,)), ((), ())), preferred_element_type=F32)
    across = lax.broadcasted_iota(jnp.int32, (count, count), 1)
    down = lax.broadcasted_iota(jnp.int32, (count, count), 0)

    def column(row):
        return jnp.sum(jnp.where(across == down, row.astype(F32), 0.0), axis=1, keepdims=True).astype(jnp.int32)

    route0 = column(routes_ref[0:1, :])
    route1 = column(routes_ref[1:2, :])
    ids = lax.broadcasted_iota(jnp.int32, (count, n), 1)
    hot0 = (ids == route0).astype(F32)
    hot1 = (ids == route1).astype(F32)
    earlier = (across < down).astype(F32).astype(BF16)
    before = jnp.dot(earlier, (hot0 + hot1).astype(BF16), preferred_element_type=F32)
    slot0 = jnp.sum(before * hot0, axis=1, keepdims=True).astype(jnp.int32)
    slot1 = jnp.sum(before * hot1, axis=1, keepdims=True).astype(jnp.int32)
    chosen0 = jnp.sum(logits * hot0, axis=1, keepdims=True)
    chosen1 = jnp.sum(logits * hot1, axis=1, keepdims=True)
    gate0 = 1.0 / (1.0 + jnp.exp(chosen1 - chosen0))
    gate1 = 1.0 - gate0
    place0 = jnp.bitwise_xor(route0, me) * cap + slot0
    place1 = jnp.bitwise_xor(route1, me) * cap + slot1
    columns = lax.broadcasted_iota(jnp.int32, (count, n * cap), 1)
    at0 = columns == place0
    at1 = columns == place1
    onehots[...] = jnp.where(at0 | at1, 1.0, 0.0).astype(BF16)

    def packed(first, last):
        picks = onehots[:, first * cap : last * cap]
        outgoing[first * cap : last * cap, :] = lax.dot_general(
            picks, normed, (((0,), (0,)), ((), ())), preferred_element_type=F32
        ).astype(BF16)

    def at(k):
        return pl.ds(pl.multiple_of(k * cap, cap), cap)

    def far_copy(k):
        return pltpu.make_async_remote_copy(
            src_ref=outgoing.at[at(k), mine], dst_ref=rows_in.at[at(k), mine],
            send_sem=disp_send.at[k], recv_sem=disp_recv.at[k],
            device_id={"expert": flip(me, k, n)}, device_id_type=MESH,
        )

    def near_copy(k):
        return pltpu.make_async_remote_copy(
            src_ref=outgoing.at[at(k)], dst_ref=rows_in.at[at(k)],
            send_sem=disp_send.at[k], recv_sem=disp_recv.at[k],
            device_id={"expert": flip(me, k, n)}, device_id_type=MESH,
        )

    packed(near, n)

    @pl.loop(near, n)
    def _(k):
        far_copy(k).start()

    packed(0, near)

    @pl.loop(1, near)
    def _(k):
        near_copy(k).start()

    rows_in[0:cap, :] = outgoing[0:cap, :]

    low = jnp.where(at0, gate0, jnp.where(at1, gate1, 0.0))
    onehots[...] = low.astype(BF16)
    rest = (low - low.astype(BF16).astype(F32)).astype(BF16)

    def span(g):
        return slice(spans[g][0] * cap, spans[g][1] * cap)

    def forward_copy(g):
        return pltpu.make_async_remote_copy(
            src_ref=rows_in.at[span(g), mine], dst_ref=rows_in.at[span(g), mine],
            send_sem=fwd_send.at[g], recv_sem=fwd_recv.at[g],
            device_id={"head": other}, device_id_type=MESH,
        )

    def reduce_copy(g):
        return pltpu.make_async_remote_copy(
            src_ref=part_out.at[span(g)], dst_ref=part_in.at[span(g)],
            send_sem=red_send.at[g], recv_sem=red_recv.at[g],
            device_id={"head": other}, device_id_type=MESH,
        )

    def return_copy(k):
        return pltpu.make_async_remote_copy(
            src_ref=summed.at[at(k)], dst_ref=back.at[at(k)],
            send_sem=ret_send.at[k], recv_sem=ret_recv.at[k],
            device_id={"expert": flip(me, k, n)}, device_id_type=MESH,
        )

    def arrive(g):
        far = spans[g][0] >= near

        @pl.loop(max(1, spans[g][0]), spans[g][1])
        def _(k):
            (far_copy if far else near_copy)(k).wait_recv()

        if far:
            forward_copy(g).start()

    def work(g):
        if g == 0:
            load_in.wait()
        if spans[g][0] >= near:
            forward_copy(g).wait_recv()
        tile = ff // 4
        size = (spans[g][1] - spans[g][0]) * cap

        @pl.loop(0, 4)
        def _(i):
            cols = pl.ds(pl.multiple_of(i * tile, tile), tile)
            value = jnp.dot(rows_in[span(g), :], w_in[:, cols], preferred_element_type=F32)
            hidden[:size, cols] = jnp.maximum(value, 0.0).astype(BF16)

        if g == 0:
            load_out.wait()
        part_out[span(g), :] = jnp.dot(hidden[:size, :], w_out[:, theirs], preferred_element_type=F32).astype(BF16)
        reduce_copy(g).start()
        part_own[span(g), :] = jnp.dot(hidden[:size, :], w_out[:, mine], preferred_element_type=F32)

    def give(g):
        reduce_copy(g).wait_recv()
        summed[span(g), :] = (part_own[span(g), :] + part_in[span(g), :].astype(F32)).astype(BF16)
        if g == 0:
            back[0:cap, :] = summed[0:cap, :]

        @pl.loop(max(1, spans[g][0]), spans[g][1])
        def _(k):
            return_copy(k).start()

    arrive(0)
    work(0)
    arrive(1)
    for g in range(1, groups):
        if g < len(bits):
            kv_wait(bits[g - 1])
            kv_start(bits[g])
        if g + 1 < groups:
            arrive(g + 1)
        work(g)
        give(g - 1)
    give(groups - 1)
    for g in range(groups, len(bits)):
        kv_wait(bits[g - 1])
        kv_start(bits[g])
    kv_wait(bits[-1])

    @pl.loop(1, n)
    def _(k):
        return_copy(k).wait_recv()

    encoded = (
        tokens_ref[:, mine].astype(F32)
        + jnp.dot(onehots[...], back[...], preferred_element_type=F32)
        + jnp.dot(rest, back[...], preferred_element_type=F32)
    )
    for q in range(half // QCOL):
        part = encoded[:, q * QCOL : (q + 1) * QCOL]
        scale = (jnp.max(jnp.abs(part), axis=1, keepdims=True) / 127.0 + 1e-06).astype(BF16).astype(F32)
        whole = jnp.clip(jnp.floor(part / scale + 0.5), -127.0, 127.0)
        cols = pl.ds(pl.multiple_of(head * half + q * QCOL, QCOL), QCOL)
        coded[:, cols] = (whole * scale).astype(BF16)
    swap = pltpu.make_async_remote_copy(
        src_ref=coded.at[:, mine], dst_ref=coded.at[:, mine],
        send_sem=code_send, recv_sem=code_recv,
        device_id={"head": other}, device_id_type=MESH,
    )
    swap.start()
    position = lax.broadcasted_iota(jnp.int32, (count, 1), 0)
    limit = jnp.zeros((count, 1), jnp.int32)
    for i in range(lengths_ref.shape[0]):
        inside = (position >= i * SLEN) & (position < (i + 1) * SLEN)
        limit = jnp.where(inside, i * SLEN + lengths_ref[i], limit)
    keep = (position < limit).astype(F32)
    part_kv[...] = jnp.dot(coded[:, mine], kv_all[mine, :], preferred_element_type=F32)

    @pl.loop(1, near)
    def _(k):
        near_copy(k).wait_send()

    @pl.loop(near, n)
    def _(k):
        far_copy(k).wait_send()

    @pl.loop(1, n)
    def _(k):
        return_copy(k).wait_send()

    for g in range(groups):
        if spans[g][0] >= near:
            forward_copy(g).wait_send()
        reduce_copy(g).wait_send()

    for bit in bits:

        @pl.loop(0, n // (2 * bit))
        def _(i, bit=bit):
            kv_copy(bit, i).wait_send()

    swap.wait()
    total = part_kv[...] + jnp.dot(coded[:, theirs], kv_all[theirs, :], preferred_element_type=F32)
    kv_ref[...] = (total * keep).astype(BF16)


def encoder(tokens, router, routes, lengths, kv_weight, w_in, w_out):
    n = lax.axis_size("expert")
    count, width = tokens.shape
    half = width // 2
    ff = w_in.shape[2]
    cap = -(-(3 * count // n) // 16) * 16
    spans = [(0, n // 4), (n // 4, n // 2)]
    spans += [(n // 2 + i * n // 8, n // 2 + (i + 1) * n // 8) for i in range(4)]
    groups = len(spans)
    slots = n * cap
    vmem = pl.BlockSpec(memory_space=pltpu.VMEM)
    anywhere = pl.BlockSpec(memory_space=pl.ANY)
    dma = pltpu.SemaphoreType.DMA
    return pl.pallas_call(
        functools.partial(kernel, n, cap, spans),
        out_shape=jax.ShapeDtypeStruct((count, kv_weight.shape[1]), BF16),
        in_specs=[
            vmem, vmem, vmem, pl.BlockSpec(memory_space=pltpu.SMEM), anywhere, anywhere, anywhere
        ],
        out_specs=vmem,
        scratch_shapes=[
            pltpu.VMEM((width, ff), BF16),
            pltpu.VMEM((ff, width), BF16),
            pltpu.VMEM((count, slots), BF16),
            pltpu.VMEM((slots, width), BF16),
            pltpu.VMEM((slots, width), BF16),
            pltpu.VMEM((slots // 4, ff), BF16),
            pltpu.VMEM((slots, half), BF16),
            pltpu.VMEM((slots, half), BF16),
            pltpu.VMEM((slots, half), F32),
            pltpu.VMEM((slots, half), BF16),
            pltpu.VMEM((slots, half), BF16),
            pltpu.VMEM((count, width), BF16),
            pltpu.VMEM((width, kv_weight.shape[1]), BF16),
            pltpu.VMEM((count, kv_weight.shape[1]), F32),
            dma((3,)),
            dma((n,)), dma((n,)),
            dma((groups,)), dma((groups,)),
            dma((groups,)), dma((groups,)),
            dma((n,)), dma((n,)),
            dma, dma,
            dma((n - 1,)), dma((n - 1,)),
        ],
        compiler_params=pltpu.CompilerParams(
            collective_id=0, has_side_effects=True, vmem_limit_bytes=58 * 1024 * 1024
        ),
        cost_estimate=pl.CostEstimate(
            flops=4 * slots * width * ff, bytes_accessed=4 * width * ff, transcendentals=0
        ),
    )(tokens, router.T, routes.T, lengths, kv_weight, w_in, w_out)


def body(tokens, router, routes, w_in, w_out, lengths, kv_weight):
    count = tokens.shape[0]
    flat = kv_weight.reshape(kv_weight.shape[0], -1)
    out = encoder(tokens, router, routes, lengths, flat, w_in, w_out)
    return out.reshape((count,) + kv_weight.shape[1:])


def solution(mesh):
    placed = (
        P(("groups", "expert"), None),
        P(),
        P(("groups", "expert"), None),
        P("expert", None, "head"),
        P("expert", "head", None),
        P(("groups", "expert")),
        P("expert", None, "head"),
    )
    return jax.shard_map(
        body,
        mesh=mesh,
        in_specs=placed,
        out_specs=P(("groups", "expert"), None, "head"),
        check_vma=False,
    )
```

```python
import functools

import jax
import jax.numpy as jnp
from jax import lax
from jax.experimental import pallas as pl
from jax.experimental.pallas import tpu as pltpu
from jax.sharding import PartitionSpec as P

QCOL = 256
SLEN = 128
MESH = pl.DeviceIdType.MESH
F32 = jnp.float32
BF16 = jnp.bfloat16


def flip(me, k, n):
    out, bit = 0, 1
    while bit < n:
        a = lax.rem(lax.div(me, jnp.int32(bit)), jnp.int32(2))
        b = lax.rem(lax.div(jnp.int32(k), jnp.int32(bit)), jnp.int32(2))
        out = out + bit * lax.rem(a + b, jnp.int32(2))
        bit *= 2
    return out


def kernel(
    n, cap, spans,
    tokens_ref, router_ref, routes_ref, lengths_ref, kv_hbm, w_in_hbm, w_out_hbm, kv_ref,
    w_in, w_out, onehots, outgoing, rows_in, hidden, part_out, part_in, part_own, summed, back, coded, kv_all, part_kv,
    w_sem, disp_send, disp_recv, fwd_send, fwd_recv, red_send, red_recv, ret_send, ret_recv, code_send, code_recv, kv_send, kv_recv,
):
    me = lax.axis_index("expert")
    head = lax.axis_index("head")
    other = 1 - head
    count, width = tokens_ref.shape
    half = width // 2
    ff = w_in.shape[1]
    groups = len(spans)
    depth = kv_hbm.shape[0]
    near = n // 2
    mine = pl.ds(pl.multiple_of(head * half, half), half)
    theirs = pl.ds(pl.multiple_of(other * half, half), half)

    load_in = pltpu.make_async_copy(w_in_hbm.at[0], w_in, w_sem.at[0])
    load_out = pltpu.make_async_copy(w_out_hbm.at[0], w_out, w_sem.at[1])

    def kv_at(expert):
        return pl.ds(pl.multiple_of(expert * depth, depth), depth)

    load_kv = pltpu.make_async_copy(kv_hbm, kv_all.at[kv_at(me)], w_sem.at[2])
    load_kv.start()
    load_in.start()
    load_out.start()

    barrier = pltpu.get_barrier_semaphore()

    @pl.loop(1, n)
    def _(k):
        pl.semaphore_signal(barrier, inc=1, device_id={"expert": flip(me, k, n)}, device_id_type=MESH)

    pl.semaphore_signal(barrier, inc=1, device_id={"head": other}, device_id_type=MESH)

    load_kv.wait()
    pl.semaphore_wait(barrier, n)

    def kv_copy(bit, i):
        owner = flip(me, i * (2 * bit), n)
        sem = n // (2 * bit) - 1 + i
        return pltpu.make_async_remote_copy(
            src_ref=kv_all.at[kv_at(owner)], dst_ref=kv_all.at[kv_at(owner)],
            send_sem=kv_send.at[sem], recv_sem=kv_recv.at[sem],
            device_id={"expert": flip(me, bit, n)}, device_id_type=MESH,
        )

    def kv_start(bit):
        @pl.loop(0, n // (2 * bit))
        def _(i):
            kv_copy(bit, i).start()

    def kv_wait(bit):
        @pl.loop(0, n // (2 * bit))
        def _(i):
            kv_copy(bit, i).wait_recv()

    bits = []
    while n >> (len(bits) + 1):
        bits.append(n >> (len(bits) + 1))
    kv_start(bits[0])

    wide = tokens_ref[...].astype(F32)
    center = jnp.mean(wide, axis=-1, keepdims=True)
    spread = jnp.mean((wide - center) ** 2, axis=-1, keepdims=True)
    normed = ((wide - center) * lax.rsqrt(spread + 1e-05)).astype(BF16)
    logits = lax.dot_general(normed, router_ref[...], (((1,), (1,)), ((), ())), preferred_element_type=F32)
    across = lax.broadcasted_iota(jnp.int32, (count, count), 1)
    down = lax.broadcasted_iota(jnp.int32, (count, count), 0)

    def column(row):
        return jnp.sum(jnp.where(across == down, row.astype(F32), 0.0), axis=1, keepdims=True).astype(jnp.int32)

    route0 = column(routes_ref[0:1, :])
    route1 = column(routes_ref[1:2, :])
    ids = lax.broadcasted_iota(jnp.int32, (count, n), 1)
    hot0 = (ids == route0).astype(F32)
    hot1 = (ids == route1).astype(F32)
    earlier = (across < down).astype(F32).astype(BF16)
    before = jnp.dot(earlier, (hot0 + hot1).astype(BF16), preferred_element_type=F32)
    slot0 = jnp.sum(before * hot0, axis=1, keepdims=True).astype(jnp.int32)
    slot1 = jnp.sum(before * hot1, axis=1, keepdims=True).astype(jnp.int32)
    chosen0 = jnp.sum(logits * hot0, axis=1, keepdims=True)
    chosen1 = jnp.sum(logits * hot1, axis=1, keepdims=True)
    gate0 = 1.0 / (1.0 + jnp.exp(chosen1 - chosen0))
    gate1 = 1.0 - gate0
    place0 = jnp.bitwise_xor(route0, me) * cap + slot0
    place1 = jnp.bitwise_xor(route1, me) * cap + slot1
    columns = lax.broadcasted_iota(jnp.int32, (count, n * cap), 1)
    at0 = columns == place0
    at1 = columns == place1
    onehots[...] = jnp.where(at0 | at1, 1.0, 0.0).astype(BF16)

    def packed(first, last):
        picks = onehots[:, first * cap : last * cap]
        outgoing[first * cap : last * cap, :] = lax.dot_general(
            picks, normed, (((0,), (0,)), ((), ())), preferred_element_type=F32
        ).astype(BF16)

    def at(k):
        return pl.ds(pl.multiple_of(k * cap, cap), cap)

    def far_copy(k):
        return pltpu.make_async_remote_copy(
            src_ref=outgoing.at[at(k), mine], dst_ref=rows_in.at[at(k), mine],
            send_sem=disp_send.at[k], recv_sem=disp_recv.at[k],
            device_id={"expert": flip(me, k, n)}, device_id_type=MESH,
        )

    def near_copy(k):
        return pltpu.make_async_remote_copy(
            src_ref=outgoing.at[at(k)], dst_ref=rows_in.at[at(k)],
            send_sem=disp_send.at[k], recv_sem=disp_recv.at[k],
            device_id={"expert": flip(me, k, n)}, device_id_type=MESH,
        )

    packed(near, n)

    packed(0, near)

    @pl.loop(1, near)
    def _(k):
        near_copy(k).start()

    @pl.loop(near, n)
    def _(k):
        far_copy(k).start()

    rows_in[0:cap, :] = outgoing[0:cap, :]

    low = jnp.where(at0, gate0, jnp.where(at1, gate1, 0.0))
    onehots[...] = low.astype(BF16)
    rest = (low - low.astype(BF16).astype(F32)).astype(BF16)

    def span(g):
        return slice(spans[g][0] * cap, spans[g][1] * cap)

    def forward_copy(g):
        return pltpu.make_async_remote_copy(
            src_ref=rows_in.at[span(g), mine], dst_ref=rows_in.at[span(g), mine],
            send_sem=fwd_send.at[g], recv_sem=fwd_recv.at[g],
            device_id={"head": other}, device_id_type=MESH,
        )

    def reduce_copy(g):
        return pltpu.make_async_remote_copy(
            src_ref=part_out.at[span(g)], dst_ref=part_in.at[span(g)],
            send_sem=red_send.at[g], recv_sem=red_recv.at[g],
            device_id={"head": other}, device_id_type=MESH,
        )

    def return_copy(k):
        return pltpu.make_async_remote_copy(
            src_ref=summed.at[at(k)], dst_ref=back.at[at(k)],
            send_sem=ret_send.at[k], recv_sem=ret_recv.at[k],
            device_id={"expert": flip(me, k, n)}, device_id_type=MESH,
        )

    def arrive(g):
        far = spans[g][0] >= near

        @pl.loop(max(1, spans[g][0]), spans[g][1])
        def _(k):
            (far_copy if far else near_copy)(k).wait_recv()

        if far:
            forward_copy(g).start()

    def work(g):
        if g == 0:
            load_in.wait()
        if spans[g][0] >= near:
            forward_copy(g).wait_recv()
        tile = ff // 4
        size = (spans[g][1] - spans[g][0]) * cap

        @pl.loop(0, 4)
        def _(i):
            cols = pl.ds(pl.multiple_of(i * tile, tile), tile)
            value = jnp.dot(rows_in[span(g), :], w_in[:, cols], preferred_element_type=F32)
            hidden[:size, cols] = jnp.maximum(value, 0.0).astype(BF16)

        if g == 0:
            load_out.wait()
        part_out[span(g), :] = jnp.dot(hidden[:size, :], w_out[:, theirs], preferred_element_type=F32).astype(BF16)
        reduce_copy(g).start()
        part_own[span(g), :] = jnp.dot(hidden[:size, :], w_out[:, mine], preferred_element_type=F32)

    def give(g):
        reduce_copy(g).wait_recv()
        summed[span(g), :] = (part_own[span(g), :] + part_in[span(g), :].astype(F32)).astype(BF16)
        if g == 0:
            back[0:cap, :] = summed[0:cap, :]

        @pl.loop(max(1, spans[g][0]), spans[g][1])
        def _(k):
            return_copy(k).start()

    arrive(0)
    work(0)
    arrive(1)
    for g in range(1, groups):
        if g < len(bits):
            kv_wait(bits[g - 1])
            kv_start(bits[g])
        if g + 1 < groups:
            arrive(g + 1)
        work(g)
        give(g - 1)
    give(groups - 1)
    for g in range(groups, len(bits)):
        kv_wait(bits[g - 1])
        kv_start(bits[g])
    kv_wait(bits[-1])

    @pl.loop(1, n)
    def _(k):
        return_copy(k).wait_recv()

    encoded = (
        tokens_ref[:, mine].astype(F32)
        + jnp.dot(onehots[...], back[...], preferred_element_type=F32)
        + jnp.dot(rest, back[...], preferred_element_type=F32)
    )
    for q in range(half // QCOL):
        part = encoded[:, q * QCOL : (q + 1) * QCOL]
        scale = (jnp.max(jnp.abs(part), axis=1, keepdims=True) / 127.0 + 1e-06).astype(BF16).astype(F32)
        whole = jnp.clip(jnp.floor(part / scale + 0.5), -127.0, 127.0)
        cols = pl.ds(pl.multiple_of(head * half + q * QCOL, QCOL), QCOL)
        coded[:, cols] = (whole * scale).astype(BF16)
    swap = pltpu.make_async_remote_copy(
        src_ref=coded.at[:, mine], dst_ref=coded.at[:, mine],
        send_sem=code_send, recv_sem=code_recv,
        device_id={"head": other}, device_id_type=MESH,
    )
    swap.start()
    position = lax.broadcasted_iota(jnp.int32, (count, 1), 0)
    limit = jnp.zeros((count, 1), jnp.int32)
    for i in range(lengths_ref.shape[0]):
        inside = (position >= i * SLEN) & (position < (i + 1) * SLEN)
        limit = jnp.where(inside, i * SLEN + lengths_ref[i], limit)
    keep = (position < limit).astype(F32)
    part_kv[...] = jnp.dot(coded[:, mine], kv_all[mine, :], preferred_element_type=F32)

    @pl.loop(1, near)
    def _(k):
        near_copy(k).wait_send()

    @pl.loop(near, n)
    def _(k):
        far_copy(k).wait_send()

    @pl.loop(1, n)
    def _(k):
        return_copy(k).wait_send()

    for g in range(groups):
        if spans[g][0] >= near:
            forward_copy(g).wait_send()
        reduce_copy(g).wait_send()

    for bit in bits:

        @pl.loop(0, n // (2 * bit))
        def _(i, bit=bit):
            kv_copy(bit, i).wait_send()

    swap.wait()
    total = part_kv[...] + jnp.dot(coded[:, theirs], kv_all[theirs, :], preferred_element_type=F32)
    kv_ref[...] = (total * keep).astype(BF16)


def encoder(tokens, router, routes, lengths, kv_weight, w_in, w_out):
    n = lax.axis_size("expert")
    count, width = tokens.shape
    half = width // 2
    ff = w_in.shape[2]
    cap = -(-(3 * count // n) // 16) * 16
    spans = [(0, n // 4), (n // 4, n // 2)]
    spans += [(n // 2 + i * n // 8, n // 2 + (i + 1) * n // 8) for i in range(4)]
    groups = len(spans)
    slots = n * cap
    vmem = pl.BlockSpec(memory_space=pltpu.VMEM)
    anywhere = pl.BlockSpec(memory_space=pl.ANY)
    dma = pltpu.SemaphoreType.DMA
    return pl.pallas_call(
        functools.partial(kernel, n, cap, spans),
        out_shape=jax.ShapeDtypeStruct((count, kv_weight.shape[1]), BF16),
        in_specs=[
            vmem, vmem, vmem, pl.BlockSpec(memory_space=pltpu.SMEM), anywhere, anywhere, anywhere
        ],
        out_specs=vmem,
        scratch_shapes=[
            pltpu.VMEM((width, ff), BF16),
            pltpu.VMEM((ff, width), BF16),
            pltpu.VMEM((count, slots), BF16),
            pltpu.VMEM((slots, width), BF16),
            pltpu.VMEM((slots, width), BF16),
            pltpu.VMEM((slots // 4, ff), BF16),
            pltpu.VMEM((slots, half), BF16),
            pltpu.VMEM((slots, half), BF16),
            pltpu.VMEM((slots, half), F32),
            pltpu.VMEM((slots, half), BF16),
            pltpu.VMEM((slots, half), BF16),
            pltpu.VMEM((count, width), BF16),
            pltpu.VMEM((width, kv_weight.shape[1]), BF16),
            pltpu.VMEM((count, kv_weight.shape[1]), F32),
            dma((3,)),
            dma((n,)), dma((n,)),
            dma((groups,)), dma((groups,)),
            dma((groups,)), dma((groups,)),
            dma((n,)), dma((n,)),
            dma, dma,
            dma((n - 1,)), dma((n - 1,)),
        ],
        compiler_params=pltpu.CompilerParams(
            collective_id=0, has_side_effects=True, vmem_limit_bytes=58 * 1024 * 1024
        ),
        cost_estimate=pl.CostEstimate(
            flops=4 * slots * width * ff, bytes_accessed=4 * width * ff, transcendentals=0
        ),
    )(tokens, router.T, routes.T, lengths, kv_weight, w_in, w_out)


def body(tokens, router, routes, w_in, w_out, lengths, kv_weight):
    count = tokens.shape[0]
    flat = kv_weight.reshape(kv_weight.shape[0], -1)
    out = encoder(tokens, router, routes, lengths, flat, w_in, w_out)
    return out.reshape((count,) + kv_weight.shape[1:])


def solution(mesh):
    placed = (
        P(("groups", "expert"), None),
        P(),
        P(("groups", "expert"), None),
        P("expert", None, "head"),
        P("expert", "head", None),
        P(("groups", "expert")),
        P("expert", None, "head"),
    )
    return jax.shard_map(
        body,
        mesh=mesh,
        in_specs=placed,
        out_specs=P(("groups", "expert"), None, "head"),
        check_vma=False,
    )
```
